128 devices in a mesh: wide: 16 (over z_hi, y, core), narrow: 8 (over z_lo, x).
Axes of the slice: x: 4, y: 4, z: 4 (z_hi: 2, z_lo: 2; z = z_hi * 2 + z_lo), core: 2. Of those that a mesh axis runs over, the one named last changes fastest.
Arguments:
- state: float32 [16, 8, 524288], P('wide', 'narrow'), may hold values from -6 to 6
- angles: float32 [6, 2, 7], replicated, may hold values from -3.140625 to 3.140625
- cz_pairs: int32 [6, 12, 2], replicated, may hold values from 0 to 18
Outputs:
- final_state: float32 [16, 8, 524288], P('wide', 'narrow')
The draws below stay inside these ranges and needn't reach their ends.
All inputs are finite; a program needn't handle non-finite values.
Results may differ from the reference program's by a relative error of at most 0.0003.
Values sent between devices are 32-bit elements; how exact they have to be, the bound alone decides.
A program may use at most 64 MiB of HBM per device.

```python
import jax
import jax.numpy as jnp
from jax import lax

LOCALQ = 19
SLAB = 524288
ROUNDS = 6
PAIRS = 12
BLOCK = 7
N_WIDE = 16
N_NARROW = 8


def touch_ends(entries, key, least, high):
    spot = [jax.random.randint(jax.random.fold_in(key, axis), (), 0, length) for axis, length in enumerate(entries.shape)]
    main_axis = entries.shape.index(max(entries.shape))
    neighbour = spot[:main_axis] + [(spot[main_axis] + 1) % entries.shape[main_axis]] + spot[main_axis + 1:]
    return entries.at[tuple(spot)].set(least).at[tuple(neighbour)].set(high)


def block_scale(rng, dims, pieces, least, largest):
    loudness, own = 1.0, jax.random.fold_in(rng, 6)
    for axis_at, parts in pieces:
        heights = jnp.exp(jax.random.uniform(jax.random.fold_in(own, axis_at), (parts,), jnp.float32, least / len(pieces), largest / len(pieces)))
        loudness = loudness * jnp.repeat(heights, dims[axis_at] // parts).reshape([-1 if axis == axis_at else 1 for axis in range(len(dims))])
    return loudness


def scatter_about(rng, shape, spread, bound, pieces=(), held_as=jnp.bfloat16):
    result = spread * jax.random.normal(rng, shape, jnp.float32)
    if pieces:
        result = result * block_scale(rng, shape, pieces, -0.22, 0.18)
    return jnp.clip(result, -bound, bound).astype(held_as)


def setup_inputs(seed: int = 0) -> dict:
    seeds = jax.random.split(jax.random.key(seed), 4)
    state = scatter_about(seeds[0], (N_WIDE, N_NARROW, SLAB), 1.0, 6.0, ((0, 16), (1, 8)), jnp.float32)
    angles = jnp.clip(jax.random.uniform(seeds[1], (ROUNDS, 2, BLOCK), jnp.float32, -3.140625, 3.140625), -3.140625, 3.140625)
    cz_pairs = touch_ends(jax.random.randint(seeds[2], (ROUNDS, PAIRS, 2), 0, LOCALQ), jax.random.fold_in(seeds[2], 1), 0, LOCALQ - 1).astype(jnp.int32)
    return {"state": state, "angles": angles, "cz_pairs": cz_pairs}


def block_matrix(thetas):
    rows = jnp.arange(128, dtype=jnp.int32)[:, None]
    cols = jnp.arange(128, dtype=jnp.int32)[None, :]
    matrix = jnp.ones((128, 128), jnp.float32)
    for qubit in range(7):
        row_bit = (rows >> qubit) & 1
        col_bit = (cols >> qubit) & 1
        cosine = jnp.cos(thetas[qubit] * 0.5)
        sine = jnp.sin(thetas[qubit] * 0.5)
        factor = jnp.where(row_bit == col_bit, cosine, jnp.where(row_bit == 1, sine, -sine))
        matrix = matrix * factor
    return matrix


def phase_signs(pairs, count):
    index = jnp.arange(count, dtype=jnp.int32)
    parity = jnp.zeros((count,), jnp.int32)
    for pair_no in range(pairs.shape[0]):
        first = jnp.right_shift(index, pairs[pair_no, 0]) & 1
        second = jnp.right_shift(index, pairs[pair_no, 1]) & 1
        parity = parity ^ (first & second)
    return (1 - 2 * parity).astype(jnp.float32)


def reference(state, angles, cz_pairs):
    slab_len = state.shape[2]
    wide_bits = N_WIDE.bit_length() - 1
    narrow_bits = N_NARROW.bit_length() - 1
    amplitudes = state
    for step_no in range(ROUNDS):
        first_gate = block_matrix(angles[step_no, 0])
        second_gate = block_matrix(angles[step_no, 1])
        rows = jnp.dot(amplitudes.reshape(-1, 128), first_gate.T, precision=lax.Precision.HIGHEST, preferred_element_type=jnp.float32)
        cube = jnp.einsum("rba,jb->rja", rows.reshape(-1, 128, 128), second_gate, precision=lax.Precision.HIGHEST)
        amplitudes = cube.reshape(N_WIDE, N_NARROW, slab_len) * phase_signs(cz_pairs[step_no], slab_len)[None, None, :]
        level = 7 + step_no % 7
        lower = 2 ** level
        upper = slab_len // (2 * lower)
        if step_no % 2 == 0:
            bit_pos = (step_no // 2) % wide_bits
            shaped = amplitudes.reshape(N_WIDE // 2 ** (bit_pos + 1), 2, 2 ** bit_pos, N_NARROW, upper, 2, lower)
            amplitudes = jnp.swapaxes(shaped, 1, 5).reshape(N_WIDE, N_NARROW, slab_len)
        else:
            bit_pos = (step_no // 2) % narrow_bits
            shaped = amplitudes.reshape(N_WIDE, N_NARROW // 2 ** (bit_pos + 1), 2, 2 ** bit_pos, upper, 2, lower)
            amplitudes = jnp.swapaxes(shaped, 2, 5).reshape(N_WIDE, N_NARROW, slab_len)
    return amplitudes
```

```python
import functools

import jax
import jax.numpy as jnp
from jax import lax
from jax.experimental import pallas as pl
from jax.experimental.pallas import tpu as pltpu
from jax.sharding import PartitionSpec as P

MESH = pl.DeviceIdType.MESH
F32 = jnp.float32
BF16 = jnp.bfloat16
ROUNDS = 6
ROWS = 128
LANES = 128
HALF = 64
CHUNKS = 32
GROUP = 2
GROUPS = CHUNKS // GROUP
LAG = 1


def trade_bit(k, wide, narrow):
    level = k // 2
    step = jnp.where(level == 0, 1, jnp.where(level == 1, 2, 4))
    index = jnp.where(k % 2 == 0, wide, narrow)
    return step, (index // step) % 2


def partner_of(k, wide, narrow):
    step, bit = trade_bit(k, wide, narrow)
    move = step * (1 - 2 * bit)
    even = 1 - k % 2
    return wide + move * even, narrow + move * (1 - even)


def row_order(pos, k, bit):
    low = pos & 63
    under = low & ((1 << k) - 1)
    over = (low >> k) << (k + 1)
    return under | over | (((pos >> 6) ^ bit) << k)


def fold_parity(bits):
    bits = bits ^ (bits >> 4)
    bits = bits ^ (bits >> 2)
    bits = bits ^ (bits >> 1)
    return bits & 1


def rotation_product(out, inp, cosines, sines, base):
    differ = out ^ inp
    value = 1 - 2 * fold_parity(inp & ~out & 127).astype(F32)
    for qubit in range(7):
        row = base + qubit
        value = value * jnp.where((differ >> qubit) & 1 == 0, cosines[row : row + 1], sines[row : row + 1])
    return value


def split(value):
    high = value.astype(BF16)
    low = (value - high.astype(F32)).astype(BF16)
    return high, low


def iota(shape, axis):
    return lax.broadcasted_iota(jnp.int32, shape, axis)


def build(k, wide, narrow, angles, pairs, right_tab, left_tab, sign_tab, row_tab, lane_tab):
    _, bit = trade_bit(k, wide, narrow)
    before = jnp.maximum(k - 1, 0)
    _, bit_before = trade_bit(before, wide, narrow)
    rows = iota((ROWS, LANES), 0)
    cols = iota((ROWS, LANES), 1)
    slot = iota((16, LANES), 0)
    half = jnp.zeros((16, LANES), F32)
    for block in range(2):
        for qubit in range(7):
            half = jnp.where(slot == block * 8 + qubit, angles[k, block, qubit] * 0.5, half)
    cosines = jnp.cos(half)
    sines = jnp.sin(half)

    high, low = split(rotation_product(cols, rows, cosines, sines, 0))
    both = jnp.concatenate([high, low], axis=1)
    right_tab[k, 0:ROWS, :] = both
    right_tab[k, ROWS : 2 * ROWS, :] = both

    out = row_order(rows, k, bit)
    inp = jnp.where(k == 0, cols, row_order(cols, before, bit_before))
    high, low = split(rotation_product(out, inp, cosines, sines, 8))
    left_tab[k, 0:ROWS, :] = jnp.concatenate([high, high], axis=1)
    left_tab[k, ROWS : 2 * ROWS, :] = jnp.concatenate([low, low], axis=1)

    def signs(index):
        parity = jnp.zeros(index.shape, jnp.int32)
        for pair in range(12):
            parity = parity ^ ((index >> pairs[k, pair, 0]) & (index >> pairs[k, pair, 1]))
        return (1 - 2 * (parity & 1)).astype(F32)

    sign_tab[k] = signs(out * 128 + cols)
    by_row = signs(out[:, :CHUNKS] * 128 + cols[:, :CHUNKS] * 16384)
    row_tab[k] = (by_row * by_row[:, 0:1]).astype(BF16)
    by_lane = signs(rows[:CHUNKS] * 16384 + cols[:CHUNKS])
    lane_tab[k] = by_lane * by_lane[0:1, :] * by_lane[:, 0:1]


def work(k, g, held, leave, right_tab, left_tab, sign_tab, row_tab, lane_tab):
    first = g * GROUP
    chunk = iota((CHUNKS, LANES), 0)
    lanes = lane_tab[k]
    picks = jnp.concatenate(
        [jnp.where(chunk == first + j, lanes, 0.0) for j in range(GROUP)], axis=1
    ).astype(BF16)
    phase = jnp.dot(row_tab[k], picks, preferred_element_type=F32)
    sign = sign_tab[k]
    results = []
    for j in range(0, GROUP, 2):
        values = held[k, pl.ds(first + j, 2)].reshape(2 * ROWS, LANES)
        high, low = split(values)
        sums = jnp.dot(jnp.concatenate([high, low], axis=1), right_tab[k], preferred_element_type=F32)
        values = sums[:, :LANES] + sums[:, LANES:]
        high, low = split(values)
        stacked = jnp.concatenate(
            [
                jnp.concatenate([high[:ROWS], high[ROWS:]], axis=1),
                jnp.concatenate([low[:ROWS], low[ROWS:]], axis=1),
            ],
            axis=0,
        )
        sums = jnp.dot(left_tab[k], stacked, preferred_element_type=F32)
        sums = sums[:ROWS] + sums[ROWS:]
        for i in range(2):
            part = slice(i * LANES, (i + 1) * LANES)
            results.append(sums[:, part] * (sign * phase[:, (j + i) * LANES : (j + i + 1) * LANES]))
    for j in range(GROUP):
        held[k + 1, first + j, 0:HALF] = results[j][:HALF]
        leave[k, first + j] = results[j][HALF:]


def kernel(
    angles, pairs, state, final, held, leave, right_tab, left_tab, sign_tab, row_tab, lane_tab, in_sem, out_sem, send_sem, recv_sem
):
    wide = lax.axis_index("wide")
    narrow = lax.axis_index("narrow")
    tables = (right_tab, left_tab, sign_tab, row_tab, lane_tab)

    def fetch(g):
        part = pl.ds(g * GROUP, GROUP)
        return pltpu.make_async_copy(state.at[part], held.at[0, part], in_sem.at[g])

    def trade(k, g):
        part = pl.ds(g * GROUP, GROUP)
        return pltpu.make_async_remote_copy(
            src_ref=leave.at[k, part],
            dst_ref=held.at[k + 1, part, HALF:ROWS],
            send_sem=send_sem.at[k],
            recv_sem=recv_sem.at[k, g],
            device_id=partner_of(k, wide, narrow),
            device_id_type=MESH,
        )

    _, last_bit = trade_bit(jnp.int32(ROUNDS - 1), wide, narrow)

    def deliver(g, side):
        part = pl.ds(g * GROUP, GROUP)
        copies = []
        for upper in range(2):
            begin = side * HALF + upper * 32
            place = upper * HALF + 32 * (last_bit * (1 - 2 * side) + side)
            copies.append(
                pltpu.make_async_copy(
                    held.at[ROUNDS, part, begin : begin + 32],
                    final.at[part, pl.ds(pl.multiple_of(place, 32), 32)],
                    out_sem,
                )
            )
        return copies

    barrier = pltpu.get_barrier_semaphore()
    for k in range(ROUNDS):
        pl.semaphore_signal(barrier, inc=1, device_id=partner_of(jnp.int32(k), wide, narrow), device_id_type=MESH)

    @pl.loop(0, GROUPS)
    def _(g):
        fetch(g).start()

    build(jnp.int32(0), wide, narrow, angles, pairs, *tables)
    pl.semaphore_wait(barrier, ROUNDS)

    @pl.loop(0, GROUPS + ROUNDS * LAG)
    def _(step):
        @pl.loop(0, ROUNDS)
        def _(k):
            g = step - k * LAG

            @pl.when((g >= 0) & (g < GROUPS))
            def _():
                @pl.when(k == 0)
                def _():
                    fetch(g).wait()

                @pl.when(k > 0)
                def _():
                    trade(jnp.maximum(k - 1, 0), g).wait_recv()

                work(k, g, held, leave, *tables)
                trade(k, g).start()

                @pl.when(k == ROUNDS - 1)
                def _():
                    for copy in deliver(g, 0):
                        copy.start()

                @pl.when((g == 0) & (k < ROUNDS - 1))
                def _():
                    build(jnp.minimum(k + 1, ROUNDS - 1), wide, narrow, angles, pairs, *tables)

        done = step - ROUNDS * LAG

        @pl.when(done >= 0)
        def _():
            trade(ROUNDS - 1, done).wait_recv()
            for copy in deliver(done, 1):
                copy.start()

    for k in range(ROUNDS):
        pltpu.make_async_remote_copy(
            src_ref=leave.at[k],
            dst_ref=held.at[k + 1, :, HALF:ROWS],
            send_sem=send_sem.at[k],
            recv_sem=recv_sem.at[k, 0],
            device_id=partner_of(jnp.int32(k), wide, narrow),
            device_id_type=MESH,
        ).wait_send()
    pltpu.make_async_copy(held.at[ROUNDS], final, out_sem).wait()


def body(state, angles, cz_pairs):
    smem = pl.BlockSpec(memory_space=pltpu.SMEM)
    hbm = pl.BlockSpec(memory_space=pl.ANY)
    result = pl.pallas_call(
        kernel,
        out_shape=jax.ShapeDtypeStruct((CHUNKS, ROWS, LANES), F32),
        in_specs=[smem, smem, hbm],
        out_specs=hbm,
        scratch_shapes=[
            pltpu.VMEM((ROUNDS + 1, CHUNKS, ROWS, LANES), F32),
            pltpu.VMEM((ROUNDS, CHUNKS, HALF, LANES), F32),
            pltpu.VMEM((ROUNDS, 2 * ROWS, 2 * LANES), BF16),
            pltpu.VMEM((ROUNDS, 2 * ROWS, 2 * LANES), BF16),
            pltpu.VMEM((ROUNDS, ROWS, LANES), F32),
            pltpu.VMEM((ROUNDS, ROWS, CHUNKS), BF16),
            pltpu.VMEM((ROUNDS, CHUNKS, LANES), F32),
            pltpu.SemaphoreType.DMA((GROUPS,)),
            pltpu.SemaphoreType.DMA,
            pltpu.SemaphoreType.DMA((ROUNDS,)),
            pltpu.SemaphoreType.DMA((ROUNDS, GROUPS)),
        ],
        compiler_params=pltpu.CompilerParams(
            collective_id=0, has_side_effects=True, vmem_limit_bytes=48 << 20
        ),
        name="circuit",
    )(angles, cz_pairs, state.reshape(CHUNKS, ROWS, LANES))
    return result.reshape(state.shape)


def solution(mesh):
    return jax.shard_map(
        body,
        mesh=mesh,
        in_specs=(P("wide", "narrow", None), P(), P()),
        out_specs=P("wide", "narrow", None),
        check_vma=False,
    )
```

```python
import functools

import jax
import jax.numpy as jnp
from jax import lax
from jax.experimental import pallas as pl
from jax.experimental.pallas import tpu as pltpu
from jax.sharding import PartitionSpec as P

MESH = pl.DeviceIdType.MESH
F32 = jnp.float32
BF16 = jnp.bfloat16
ROUNDS = 6
ROWS = 128
LANES = 128
HALF = 64
CHUNKS = 32
GROUP = 2
GROUPS = CHUNKS // GROUP
OFFSET = (0, 1, 4, 7, 11, 15, 18)
BLOCKS = (tuple(range(ROUNDS)),)


def trade_bit(k, wide, narrow):
    level = k // 2
    if isinstance(k, int):
        step, index = 1 << level, (narrow if k % 2 else wide)
    else:
        step = jnp.where(level == 0, 1, jnp.where(level == 1, 2, 4))
        index = jnp.where(k % 2 == 0, wide, narrow)
    return step, (index // step) % 2


def partner_of(k, wide, narrow):
    step, bit = trade_bit(k, wide, narrow)
    move = step * (1 - 2 * bit)
    even = 1 - k % 2
    return wide + move * even, narrow + move * (1 - even)


def row_order(pos, k, bit):
    low = pos & 63
    under = low & ((1 << k) - 1)
    over = (low >> k) << (k + 1)
    return under | over | (((pos >> 6) ^ bit) << k)


def fold_parity(bits):
    bits = bits ^ (bits >> 4)
    bits = bits ^ (bits >> 2)
    bits = bits ^ (bits >> 1)
    return bits & 1


def rotation_product(out, inp, cosines, sines, base):
    differ = out ^ inp
    value = 1 - 2 * fold_parity(inp & ~out & 127).astype(F32)
    for qubit in range(7):
        row = base + qubit
        value = value * jnp.where((differ >> qubit) & 1 == 0, cosines[row : row + 1], sines[row : row + 1])
    return value


def split(value):
    high = value.astype(BF16)
    low = (value - high.astype(F32)).astype(BF16)
    return high, low


def iota(shape, axis):
    return lax.broadcasted_iota(jnp.int32, shape, axis)


def build(k, wide, narrow, angles, pairs, right_tab, left_tab, sign_tab, row_tab, lane_tab):
    _, bit = trade_bit(k, wide, narrow)
    before = jnp.maximum(k - 1, 0)
    _, bit_before = trade_bit(before, wide, narrow)
    rows = iota((ROWS, LANES), 0)
    cols = iota((ROWS, LANES), 1)
    slot = iota((16, LANES), 0)
    half = jnp.zeros((16, LANES), F32)
    for block in range(2):
        for qubit in range(7):
            half = jnp.where(slot == block * 8 + qubit, angles[k, block, qubit] * 0.5, half)
    cosines = jnp.cos(half)
    sines = jnp.sin(half)

    high, low = split(rotation_product(cols, rows, cosines, sines, 0))
    both = jnp.concatenate([high, low], axis=1)
    right_tab[k, 0:ROWS, :] = both
    right_tab[k, ROWS : 2 * ROWS, :] = both

    out = row_order(rows, k, bit)
    inp = jnp.where(k == 0, cols, row_order(cols, before, bit_before))
    high, low = split(rotation_product(out, inp, cosines, sines, 8))
    left_tab[k, 0:ROWS, :] = jnp.concatenate([high, high], axis=1)
    left_tab[k, ROWS : 2 * ROWS, :] = jnp.concatenate([low, low], axis=1)

    def signs(index):
        parity = jnp.zeros(index.shape, jnp.int32)
        for pair in range(12):
            parity = parity ^ ((index >> pairs[k, 0, pair]) & (index >> pairs[k, 1, pair]))
        return (1 - 2 * (parity & 1)).astype(F32)

    sign_tab[k] = signs(out * 128 + cols)
    by_row = signs(out[:, :CHUNKS] * 128 + cols[:, :CHUNKS] * 16384)
    row_tab[k] = (by_row * by_row[:, 0:1]).astype(BF16)
    by_lane = signs(rows[:CHUNKS] * 16384 + cols[:CHUNKS])
    lane_tab[k] = by_lane * by_lane[0:1, :] * by_lane[:, 0:1]


def gates(taken, slot, right_tab, left_tab, sign_tab, row_tab, lane_tab):
    chunk = iota((CHUNKS, LANES), 0)
    sums = {}
    for k in taken:
        high, low = split(taken[k].reshape(GROUP * ROWS, LANES))
        sums[k] = jnp.dot(jnp.concatenate([high, low], axis=1), right_tab[k], preferred_element_type=F32)
    phase = {}
    for k in taken:
        lanes = lane_tab[k]
        picks = [jnp.where(chunk == slot[k] * GROUP + j, lanes, 0.0) for j in range(GROUP)]
        picks = jnp.concatenate(picks, axis=1).astype(BF16)
        phase[k] = jnp.dot(row_tab[k], picks, preferred_element_type=F32)
    for k in taken:
        high, low = split(sums[k][:, :LANES] + sums[k][:, LANES:])
        beside = [
            jnp.concatenate([part[j * ROWS : (j + 1) * ROWS] for j in range(GROUP)], axis=1) for part in (high, low)
        ]
        sums[k] = jnp.dot(left_tab[k], jnp.concatenate(beside, axis=0), preferred_element_type=F32)
    given = {}
    for k in taken:
        total = sums[k][:ROWS] + sums[k][ROWS:]
        sign = sign_tab[k]
        given[k] = [
            total[:, j * LANES : (j + 1) * LANES] * (sign * phase[k][:, j * LANES : (j + 1) * LANES])
            for j in range(GROUP)
        ]
    return given


def kernel(
    angles_in, pairs_in, state, final, angles, pairs, held, leave, right_tab, left_tab, sign_tab, row_tab, lane_tab,
    small_sem, in_sem, out_sem, send_sem, recv_sem
):
    wide = lax.axis_index("wide")
    narrow = lax.axis_index("narrow")
    tables = (right_tab, left_tab, sign_tab, row_tab, lane_tab)

    def fetch(g):
        part = pl.ds(g * GROUP, GROUP)
        return pltpu.make_async_copy(state.at[part], held.at[0, part], in_sem.at[g])

    def trade(k, part, g):
        return pltpu.make_async_remote_copy(
            src_ref=leave.at[k, part],
            dst_ref=held.at[k + 1, part, HALF:ROWS],
            send_sem=send_sem.at[k],
            recv_sem=recv_sem.at[k, g],
            device_id=partner_of(k, wide, narrow),
            device_id_type=MESH,
        )

    def of(g):
        return pl.ds(g * GROUP, GROUP)

    _, last_bit = trade_bit(ROUNDS - 1, wide, narrow)

    def deliver(g, side):
        copies = []
        for upper in range(2):
            begin = side * HALF + upper * 32
            place = upper * HALF + 32 * (last_bit * (1 - 2 * side) + side)
            copies.append(
                pltpu.make_async_copy(
                    held.at[ROUNDS, of(g), begin : begin + 32],
                    final.at[of(g), pl.ds(pl.multiple_of(place, 32), 32)],
                    out_sem,
                )
            )
        return copies

    small = [pltpu.make_async_copy(angles_in, angles, small_sem.at[0]), pltpu.make_async_copy(pairs_in, pairs, small_sem.at[1])]
    for copy in small:
        copy.start()
    barrier = pltpu.get_barrier_semaphore()
    for k in range(ROUNDS):
        pl.semaphore_signal(barrier, inc=1, device_id=partner_of(k, wide, narrow), device_id_type=MESH)

    @pl.loop(0, GROUPS)
    def _(g):
        fetch(g).start()

    for copy in small:
        copy.wait()
    build(jnp.int32(0), wide, narrow, angles, pairs, *tables)
    pl.semaphore_wait(barrier, ROUNDS)

    @pl.loop(0, GROUPS + OFFSET[ROUNDS])
    def _(step):
        for block in BLOCKS:
            at = {k: step - OFFSET[k] for k in block}
            for k in block:
                @pl.when((at[k] >= 0) & (at[k] < GROUPS))
                def _(k=k):
                    if k == 0:
                        fetch(at[k]).wait()
                    else:
                        trade(k - 1, of(at[k]), at[k]).wait_recv()

            slot = {k: jnp.where((at[k] >= 0) & (at[k] < GROUPS), at[k], GROUPS) for k in block}
            taken = {k: held[k, of(slot[k])] for k in block}
            given = gates(taken, slot, *tables)
            for k in block:
                for j in range(GROUP):
                    leave[k, slot[k] * GROUP + j] = given[k][j][HALF:]
                    held[k + 1, slot[k] * GROUP + j, 0:HALF] = given[k][j][:HALF]
            for k in block:
                @pl.when((at[k] >= 0) & (at[k] < GROUPS))
                def _(k=k):
                    trade(k, of(at[k]), at[k]).start()
                    if k == ROUNDS - 1:
                        for copy in deliver(at[k], 0):
                            copy.start()

        @pl.when(step < ROUNDS - 1)
        def _():
            build(jnp.minimum(step + 1, ROUNDS - 1), wide, narrow, angles, pairs, *tables)

        done = step - OFFSET[ROUNDS]

        @pl.when(done >= 0)
        def _():
            trade(ROUNDS - 1, of(done), done).wait_recv()
            for copy in deliver(done, 1):
                copy.start()

    for k in range(ROUNDS):
        trade(k, slice(0, CHUNKS), 0).wait_send()
    pltpu.make_async_copy(held.at[ROUNDS, 0:CHUNKS], final, out_sem).wait()


def body(state, angles, cz_pairs):
    hbm = pl.BlockSpec(memory_space=pltpu.HBM)
    result = pl.pallas_call(
        kernel,
        out_shape=jax.ShapeDtypeStruct((CHUNKS, ROWS, LANES), F32),
        in_specs=[hbm, hbm, hbm],
        out_specs=pl.BlockSpec(memory_space=pl.ANY),
        scratch_shapes=[
            pltpu.SMEM((ROUNDS, 2, 7), F32),
            pltpu.SMEM((ROUNDS, 2, 12), jnp.int32),
            pltpu.VMEM((ROUNDS + 1, CHUNKS + GROUP, ROWS, LANES), F32),
            pltpu.VMEM((ROUNDS, CHUNKS + GROUP, HALF, LANES), F32),
            pltpu.VMEM((ROUNDS, 2 * ROWS, 2 * LANES), BF16),
            pltpu.VMEM((ROUNDS, 2 * ROWS, 2 * LANES), BF16),
            pltpu.VMEM((ROUNDS, ROWS, LANES), F32),
            pltpu.VMEM((ROUNDS, ROWS, CHUNKS), BF16),
            pltpu.VMEM((ROUNDS, CHUNKS, LANES), F32),
            pltpu.SemaphoreType.DMA((2,)),
            pltpu.SemaphoreType.DMA((GROUPS,)),
            pltpu.SemaphoreType.DMA,
            pltpu.SemaphoreType.DMA((ROUNDS,)),
            pltpu.SemaphoreType.DMA((ROUNDS, GROUPS)),
        ],
        compiler_params=pltpu.CompilerParams(
            collective_id=0, has_side_effects=True, vmem_limit_bytes=48 << 20
        ),
        name="circuit",
    )(*[pltpu.with_memory_space_constraint(v, pltpu.HBM) for v in (angles, cz_pairs.transpose(0, 2, 1))], pltpu.with_memory_space_constraint(state.reshape(CHUNKS, ROWS, LANES), pltpu.HBM))
    return result.reshape(state.shape)


def solution(mesh):
    return jax.shard_map(
        body,
        mesh=mesh,
        in_specs=(P("wide", "narrow", None), P(), P()),
        out_specs=P("wide", "narrow", None),
        check_vma=False,
    )
```

```python
import functools

import jax
import jax.numpy as jnp
from jax import lax
from jax.experimental import pallas as pl
from jax.experimental.pallas import tpu as pltpu
from jax.sharding import PartitionSpec as P

MESH = pl.DeviceIdType.MESH
F32 = jnp.float32
BF16 = jnp.bfloat16
ROUNDS = 6
ROWS = 128
LANES = 128
HALF = 64
CHUNKS = 32
GROUP = 2
GROUPS = CHUNKS // GROUP
TWICE = (3, 4)
OFFSET = (0, 2, 6, 10, 14, 18)
BLOCKS = (tuple(range(ROUNDS)),)


def trade_bit(k, wide, narrow):
    level = k // 2
    if isinstance(k, int):
        step, index = 1 << level, (narrow if k % 2 else wide)
    else:
        step = jnp.where(level == 0, 1, jnp.where(level == 1, 2, 4))
        index = jnp.where(k % 2 == 0, wide, narrow)
    return step, (index // step) % 2


def partner_of(k, wide, narrow):
    step, bit = trade_bit(k, wide, narrow)
    move = step * (1 - 2 * bit)
    return (wide, narrow + move) if k % 2 else (wide + move, narrow)


def beyond(k, wide, narrow):
    return partner_of(k, *partner_of(k - 2, wide, narrow))


def row_order(pos, k, bit):
    low = pos & 63
    under = low & ((1 << k) - 1)
    over = (low >> k) << (k + 1)
    return under | over | (((pos >> 6) ^ bit) << k)


def fold_parity(bits):
    bits = bits ^ (bits >> 4)
    bits = bits ^ (bits >> 2)
    bits = bits ^ (bits >> 1)
    return bits & 1


def rotation_product(out, inp, cosines, sines, base):
    differ = out ^ inp
    value = 1 - 2 * fold_parity(inp & ~out & 127).astype(F32)
    for qubit in range(7):
        row = base + qubit
        value = value * jnp.where((differ >> qubit) & 1 == 0, cosines[row : row + 1], sines[row : row + 1])
    return value


def split(value):
    high = value.astype(BF16)
    low = (value - high.astype(F32)).astype(BF16)
    return high, low


def iota(shape, axis):
    return lax.broadcasted_iota(jnp.int32, shape, axis)


def build(k, wide, narrow, angles, pairs, right_tab, left_tab, sign_tab, row_tab, lane_tab):
    _, bit = trade_bit(k, wide, narrow)
    before = jnp.maximum(k - 1, 0)
    _, bit_before = trade_bit(before, wide, narrow)
    rows = iota((ROWS, LANES), 0)
    cols = iota((ROWS, LANES), 1)
    slot = iota((16, LANES), 0)
    half = jnp.zeros((16, LANES), F32)
    for block in range(2):
        for qubit in range(7):
            half = jnp.where(slot == block * 8 + qubit, angles[k, block, qubit] * 0.5, half)
    cosines = jnp.cos(half)
    sines = jnp.sin(half)

    high, low = split(rotation_product(cols, rows, cosines, sines, 0))
    both = jnp.concatenate([high, low], axis=1)
    right_tab[k, 0:ROWS, :] = both
    right_tab[k, ROWS : 2 * ROWS, :] = both

    out = row_order(rows, k, bit ^ jnp.where((k == 1) | (k == 2), 1, 0))
    inp = jnp.where(k == 0, cols, row_order(cols, before, bit_before))
    high, low = split(rotation_product(out, inp, cosines, sines, 8))
    left_tab[k, 0:ROWS, :] = jnp.concatenate([high, high], axis=1)
    left_tab[k, ROWS : 2 * ROWS, :] = jnp.concatenate([low, low], axis=1)

    def signs(index):
        parity = jnp.zeros(index.shape, jnp.int32)
        for pair in range(12):
            parity = parity ^ ((index >> pairs[k, 0, pair]) & (index >> pairs[k, 1, pair]))
        return (1 - 2 * (parity & 1)).astype(F32)

    sign_tab[k] = signs(out * 128 + cols)
    by_row = signs(out[:, :CHUNKS] * 128 + cols[:, :CHUNKS] * 16384)
    row_tab[k] = (by_row * by_row[:, 0:1]).astype(BF16)
    by_lane = signs(rows[:CHUNKS] * 16384 + cols[:CHUNKS])
    lane_tab[k] = by_lane * by_lane[0:1, :] * by_lane[:, 0:1]


def gates(taken, slot, right_tab, left_tab, sign_tab, row_tab, lane_tab):
    chunk = iota((CHUNKS, LANES), 0)
    sums = {}
    for k in taken:
        high, low = split(taken[k].reshape(GROUP * ROWS, LANES))
        sums[k] = jnp.dot(jnp.concatenate([high, low], axis=1), right_tab[k], preferred_element_type=F32)
    phase = {}
    for k in taken:
        lanes = lane_tab[k]
        picks = [jnp.where(chunk == slot[k] * GROUP + j, lanes, 0.0) for j in range(GROUP)]
        picks = jnp.concatenate(picks, axis=1).astype(BF16)
        phase[k] = jnp.dot(row_tab[k], picks, preferred_element_type=F32)
    for k in taken:
        high, low = split(sums[k][:, :LANES] + sums[k][:, LANES:])
        beside = [
            jnp.concatenate([part[j * ROWS : (j + 1) * ROWS] for j in range(GROUP)], axis=1) for part in (high, low)
        ]
        sums[k] = jnp.dot(left_tab[k], jnp.concatenate(beside, axis=0), preferred_element_type=F32)
    given = {}
    for k in taken:
        total = sums[k][:ROWS] + sums[k][ROWS:]
        sign = sign_tab[k]
        given[k] = [
            total[:, j * LANES : (j + 1) * LANES] * (sign * phase[k][:, j * LANES : (j + 1) * LANES])
            for j in range(GROUP)
        ]
    return given


def kernel(
    angles_in, pairs_in, state, final, angles, pairs, held, leave, right_tab, left_tab, sign_tab, row_tab, lane_tab,
    small_sem, in_sem, out_sem, last_sem, send_sem, recv_sem
):
    wide = lax.axis_index("wide")
    narrow = lax.axis_index("narrow")
    tables = (right_tab, left_tab, sign_tab, row_tab, lane_tab)

    def fetch(g):
        part = pl.ds(g * GROUP, GROUP)
        return pltpu.make_async_copy(state.at[part], held.at[0, part], in_sem.at[g])

    def send(k, part, side, recv, device):
        return pltpu.make_async_remote_copy(
            src_ref=leave.at[k, part, side * HALF : (side + 1) * HALF],
            dst_ref=held.at[k + 1, part, side * HALF : (side + 1) * HALF],
            send_sem=send_sem.at[k],
            recv_sem=recv,
            device_id=device,
            device_id_type=MESH,
        )

    def trade(k, g):
        part, recv = of(g), recv_sem.at[k, g]
        if k in TWICE:
            return [
                send(k, part, 0, recv, partner_of(k - 2, wide, narrow)),
                send(k, part, 1, recv, beyond(k, wide, narrow)),
            ]
        if k < ROUNDS - 1:
            return [send(k, part, 1, recv, partner_of(k, wide, narrow))]
        return [
            pltpu.make_async_remote_copy(
                src_ref=leave.at[k, part, HALF + 32 * upper : HALF + 32 * upper + 32],
                dst_ref=final.at[part, pl.ds(pl.multiple_of(upper * HALF + 32 * last_bit, 32), 32)],
                send_sem=send_sem.at[k],
                recv_sem=last_sem,
                device_id=partner_of(k, wide, narrow),
                device_id_type=MESH,
            )
            for upper in range(2)
        ]

    def arrived(k, g):
        rows = slice(0, ROWS) if k in TWICE else slice(HALF, ROWS)
        pltpu.make_async_copy(leave.at[k, of(g), rows], held.at[k + 1, of(g), rows], recv_sem.at[k, g]).wait()

    def of(g):
        return pl.ds(g * GROUP, GROUP)

    _, last_bit = trade_bit(ROUNDS - 1, wide, narrow)

    def deliver(g):
        return [
            pltpu.make_async_copy(
                leave.at[ROUNDS - 1, of(g), 32 * upper : 32 * upper + 32],
                final.at[of(g), pl.ds(pl.multiple_of(upper * HALF + 32 * last_bit, 32), 32)],
                out_sem,
            )
            for upper in range(2)
        ]

    small = [pltpu.make_async_copy(angles_in, angles, small_sem.at[0]), pltpu.make_async_copy(pairs_in, pairs, small_sem.at[1])]
    for copy in small:
        copy.start()
    barrier = pltpu.get_barrier_semaphore()
    for k in range(ROUNDS):
        greeted = beyond(k, wide, narrow) if k in TWICE else partner_of(k, wide, narrow)
        pl.semaphore_signal(barrier, inc=1, device_id=greeted, device_id_type=MESH)

    @pl.loop(0, GROUPS)
    def _(g):
        fetch(g).start()

    for copy in small:
        copy.wait()
    build(jnp.int32(0), wide, narrow, angles, pairs, *tables)

    @pl.loop(0, GROUPS + OFFSET[ROUNDS - 1])
    def _(step):
        for block in BLOCKS:
            at = {k: step - OFFSET[k] for k in block}
            for k in block:
                @pl.when((at[k] >= 0) & (at[k] < GROUPS))
                def _(k=k):
                    if k == 0:
                        fetch(at[k]).wait()
                    else:
                        arrived(k - 1, at[k])

            slot = {k: jnp.where((at[k] >= 0) & (at[k] < GROUPS), at[k], GROUPS) for k in block}
            taken = {k: held[k, of(slot[k])] for k in block}
            given = gates(taken, slot, *tables)
            for k in block:
                for j in range(GROUP):
                    if k in TWICE or k == ROUNDS - 1:
                        leave[k, slot[k] * GROUP + j] = given[k][j]
                    else:
                        leave[k, slot[k] * GROUP + j, HALF:ROWS] = given[k][j][HALF:]
                        held[k + 1, slot[k] * GROUP + j, 0:HALF] = given[k][j][:HALF]
            if 0 in block:
                @pl.when(step == 0)
                def _():
                    pl.semaphore_wait(barrier, ROUNDS)

            for k in block:
                @pl.when((at[k] >= 0) & (at[k] < GROUPS))
                def _(k=k):
                    for copy in trade(k, at[k]) + (deliver(at[k]) if k == ROUNDS - 1 else []):
                        copy.start()

        @pl.when(step < ROUNDS - 1)
        def _():
            build(jnp.minimum(step + 1, ROUNDS - 1), wide, narrow, angles, pairs, *tables)

    for k in range(ROUNDS):
        rows = slice(0, ROWS) if k in TWICE else slice(HALF, ROWS)
        sent = leave.at[k, 0:CHUNKS, rows]
        pltpu.make_async_copy(sent, sent, send_sem.at[k]).wait()
    lower = leave.at[ROUNDS - 1, 0:CHUNKS, 0:HALF]
    pltpu.make_async_copy(lower, lower, out_sem).wait()
    pltpu.make_async_copy(lower, lower, last_sem).wait()


def body(state, angles, cz_pairs):
    hbm = pl.BlockSpec(memory_space=pltpu.HBM)
    result = pl.pallas_call(
        kernel,
        out_shape=jax.ShapeDtypeStruct((CHUNKS, ROWS, LANES), F32),
        in_specs=[hbm, hbm, hbm],
        out_specs=pl.BlockSpec(memory_space=pl.ANY),
        scratch_shapes=[
            pltpu.SMEM((ROUNDS, 2, 7), F32),
            pltpu.SMEM((ROUNDS, 2, 12), jnp.int32),
            pltpu.VMEM((ROUNDS, CHUNKS + GROUP, ROWS, LANES), F32),
            pltpu.VMEM((ROUNDS, CHUNKS + GROUP, ROWS, LANES), F32),
            pltpu.VMEM((ROUNDS, 2 * ROWS, 2 * LANES), BF16),
            pltpu.VMEM((ROUNDS, 2 * ROWS, 2 * LANES), BF16),
            pltpu.VMEM((ROUNDS, ROWS, LANES), F32),
            pltpu.VMEM((ROUNDS, ROWS, CHUNKS), BF16),
            pltpu.VMEM((ROUNDS, CHUNKS, LANES), F32),
            pltpu.SemaphoreType.DMA((2,)),
            pltpu.SemaphoreType.DMA((GROUPS,)),
            pltpu.SemaphoreType.DMA,
            pltpu.SemaphoreType.DMA,
            pltpu.SemaphoreType.DMA((ROUNDS,)),
            pltpu.SemaphoreType.DMA((ROUNDS - 1, GROUPS)),
        ],
        compiler_params=pltpu.CompilerParams(
            collective_id=0, has_side_effects=True, vmem_limit_bytes=48 << 20
        ),
        name="circuit",
    )(*[pltpu.with_memory_space_constraint(v, pltpu.HBM) for v in (angles, cz_pairs.transpose(0, 2, 1))], pltpu.with_memory_space_constraint(state.reshape(CHUNKS, ROWS, LANES), pltpu.HBM))
    return result.reshape(state.shape)


def solution(mesh):
    return jax.shard_map(
        body,
        mesh=mesh,
        in_specs=(P("wide", "narrow", None), P(), P()),
        out_specs=P("wide", "narrow", None),
        check_vma=False,
    )
```

```python
import functools

import jax
import jax.numpy as jnp
from jax import lax
from jax.experimental import pallas as pl
from jax.experimental.pallas import tpu as pltpu
from jax.sharding import PartitionSpec as P

MESH = pl.DeviceIdType.MESH
F32 = jnp.float32
BF16 = jnp.bfloat16
ROUNDS = 6
ROWS = 128
LANES = 128
HALF = 64
CHUNKS = 32
GROUP = 1
GROUPS = CHUNKS // GROUP
TWICE = (3, 4)
OFFSET = (0, 2, 8, 14, 20, 26)
ORDER = (0, 1, 2, 3, 4, 5)
BUILD = (0, 1, 8, 14, 20, 26)


def trade_bit(k, wide, narrow):
    step, index = 1 << k // 2, (narrow if k % 2 else wide)
    return step, (index // step) % 2


def partner_of(k, wide, narrow):
    step, bit = trade_bit(k, wide, narrow)
    move = step * (1 - 2 * bit)
    return (wide, narrow + move) if k % 2 else (wide + move, narrow)


def beyond(k, wide, narrow):
    return partner_of(k, *partner_of(k - 2, wide, narrow))


def row_order(pos, k, bit):
    low = pos & 63
    under = low & ((1 << k) - 1)
    over = (low >> k) << (k + 1)
    return under | over | (((pos >> 6) ^ bit) << k)


def fold_parity(bits):
    bits = bits ^ (bits >> 4)
    bits = bits ^ (bits >> 2)
    bits = bits ^ (bits >> 1)
    return bits & 1


def rotation_product(out, inp, cosines, sines, base):
    differ = out ^ inp
    value = 1 - 2 * fold_parity(inp & ~out & 127).astype(F32)
    for qubit in range(7):
        row = base + qubit
        value = value * jnp.where((differ >> qubit) & 1 == 0, cosines[row : row + 1], sines[row : row + 1])
    return value


def split(value):
    high = value.astype(BF16)
    low = (value - high.astype(F32)).astype(BF16)
    return high, low


def iota(shape, axis):
    return lax.broadcasted_iota(jnp.int32, shape, axis)


def build(k, wide, narrow, angles, pairs, right_tab, left_tab, sign_tab, row_tab, lane_tab):
    _, bit = trade_bit(k, wide, narrow)
    rows = iota((ROWS, LANES), 0)
    cols = iota((ROWS, LANES), 1)
    slot = iota((16, LANES), 0)
    half = jnp.zeros((16, LANES), F32)
    for block in range(2):
        for qubit in range(7):
            half = jnp.where(slot == block * 8 + qubit, angles[k, block, qubit] * 0.5, half)
    cosines = jnp.cos(half)
    sines = jnp.sin(half)

    high, low = split(rotation_product(cols, rows, cosines, sines, 0))
    both = jnp.concatenate([high, low], axis=1)
    right_tab[k, 0:ROWS, :] = both
    right_tab[k, ROWS : 2 * ROWS, :] = both

    out = row_order(rows, k, bit ^ (1 if k in (1, 2) else 0))
    inp = row_order(cols, k - 1, trade_bit(k - 1, wide, narrow)[1]) if k else cols
    high, low = split(rotation_product(out, inp, cosines, sines, 8))
    left_tab[k, 0:ROWS, :] = jnp.concatenate([high, high], axis=1)
    left_tab[k, ROWS : 2 * ROWS, :] = jnp.concatenate([low, low], axis=1)

    def signs(index):
        parity = jnp.zeros(index.shape, jnp.int32)
        for pair in range(12):
            parity = parity ^ ((index >> pairs[k, 0, pair]) & (index >> pairs[k, 1, pair]))
        return (1 - 2 * (parity & 1)).astype(F32)

    sign_tab[k] = signs(out * 128 + cols)
    by_row = signs(out[:, :CHUNKS] * 128 + cols[:, :CHUNKS] * 16384)
    row_tab[k] = (by_row * by_row[:, 0:1]).astype(BF16)
    by_lane = signs(rows[:CHUNKS] * 16384 + cols[:CHUNKS])
    lane_tab[k] = by_lane * by_lane[0:1, :] * by_lane[:, 0:1]


def gates(taken, slot, right_tab, left_tab, sign_tab, row_tab, lane_tab):
    chunk = iota((CHUNKS, LANES), 0)
    sums = {}
    for k in taken:
        high, low = split(taken[k].reshape(GROUP * ROWS, LANES))
        sums[k] = jnp.dot(jnp.concatenate([high, low], axis=1), right_tab[k], preferred_element_type=F32)
    phase = {}
    for k in taken:
        lanes = lane_tab[k]
        picks = [jnp.where(chunk == slot[k] * GROUP + j, lanes, 0.0) for j in range(GROUP)]
        picks = jnp.concatenate(picks, axis=1).astype(BF16)
        phase[k] = jnp.dot(row_tab[k], picks, preferred_element_type=F32)
    for k in taken:
        high, low = split(sums[k][:, :LANES] + sums[k][:, LANES:])
        beside = [
            jnp.concatenate([part[j * ROWS : (j + 1) * ROWS] for j in range(GROUP)], axis=1) for part in (high, low)
        ]
        sums[k] = jnp.dot(left_tab[k], jnp.concatenate(beside, axis=0), preferred_element_type=F32)
    given = {}
    for k in taken:
        total = sums[k][:ROWS] + sums[k][ROWS:]
        sign = sign_tab[k]
        given[k] = [
            total[:, j * LANES : (j + 1) * LANES] * (sign * phase[k][:, j * LANES : (j + 1) * LANES])
            for j in range(GROUP)
        ]
    return given


def kernel(
    angles_in, pairs_in, state, final, angles, pairs, held, leave, right_tab, left_tab, sign_tab, row_tab, lane_tab,
    small_sem, in_sem, out_sem, last_sem, send_sem, recv_sem
):
    wide = lax.axis_index("wide")
    narrow = lax.axis_index("narrow")
    tables = (right_tab, left_tab, sign_tab, row_tab, lane_tab)

    def fetch(g):
        part = pl.ds(g * GROUP, GROUP)
        return pltpu.make_async_copy(state.at[part], held.at[0, part], in_sem.at[g])

    def send(k, part, side, recv, device):
        return pltpu.make_async_remote_copy(
            src_ref=leave.at[k, part, side * HALF : (side + 1) * HALF],
            dst_ref=held.at[k + 1, part, side * HALF : (side + 1) * HALF],
            send_sem=send_sem.at[k],
            recv_sem=recv,
            device_id=device,
            device_id_type=MESH,
        )

    def trade(k, g):
        part, recv = of(g), recv_sem.at[k, g]
        if k in TWICE:
            return [
                send(k, part, 0, recv, partner_of(k - 2, wide, narrow)),
                send(k, part, 1, recv, beyond(k, wide, narrow)),
            ]
        if k < ROUNDS - 1:
            return [send(k, part, 1, recv, partner_of(k, wide, narrow))]
        return [
            pltpu.make_async_remote_copy(
                src_ref=leave.at[k, part, HALF + 32 * upper : HALF + 32 * upper + 32],
                dst_ref=final.at[part, pl.ds(pl.multiple_of(upper * HALF + 32 * last_bit, 32), 32)],
                send_sem=send_sem.at[k],
                recv_sem=last_sem,
                device_id=partner_of(k, wide, narrow),
                device_id_type=MESH,
            )
            for upper in range(2)
        ]

    def arrived(k, g):
        rows = slice(0, ROWS) if k in TWICE else slice(HALF, ROWS)
        pltpu.make_async_copy(leave.at[k, of(g), rows], held.at[k + 1, of(g), rows], recv_sem.at[k, g]).wait()

    def of(g):
        return pl.ds(g * GROUP, GROUP)

    _, last_bit = trade_bit(ROUNDS - 1, wide, narrow)

    def deliver(g):
        return [
            pltpu.make_async_copy(
                leave.at[ROUNDS - 1, of(g), 32 * upper : 32 * upper + 32],
                final.at[of(g), pl.ds(pl.multiple_of(upper * HALF + 32 * last_bit, 32), 32)],
                out_sem,
            )
            for upper in range(2)
        ]

    small = [pltpu.make_async_copy(angles_in, angles, small_sem.at[0]), pltpu.make_async_copy(pairs_in, pairs, small_sem.at[1])]
    for copy in small:
        copy.start()
    barrier = pltpu.get_barrier_semaphore()
    for k in range(ROUNDS):
        greeted = beyond(k, wide, narrow) if k in TWICE else partner_of(k, wide, narrow)
        pl.semaphore_signal(barrier, inc=1, device_id=greeted, device_id_type=MESH)

    @pl.loop(0, GROUPS)
    def _(g):
        fetch(g).start()

    for copy in small:
        copy.wait()
    build(0, wide, narrow, angles, pairs, *tables)
    edges = sorted({OFFSET[k] + e for k in range(ROUNDS) for e in (0, GROUPS)} | {1})
    for begin, end in zip(edges[:-1], edges[1:]):
        block = [k for k in ORDER if OFFSET[k] <= begin and end <= OFFSET[k] + GROUPS]

        @pl.loop(begin, end)
        def _(step):
            at = {k: step - OFFSET[k] for k in block}
            for k in block:
                if k == 0:
                    fetch(at[k]).wait()
                else:
                    arrived(k - 1, at[k])
            given = gates({k: held[k, of(at[k])] for k in block}, at, *tables)
            for k in block:
                for j in range(GROUP):
                    if k in TWICE or k == ROUNDS - 1:
                        leave[k, at[k] * GROUP + j] = given[k][j]
                    else:
                        leave[k, at[k] * GROUP + j, HALF:ROWS] = given[k][j][HALF:]
                        held[k + 1, at[k] * GROUP + j, 0:HALF] = given[k][j][:HALF]
            if begin == 0:
                pl.semaphore_wait(barrier, ROUNDS)
            for k in block:
                for copy in trade(k, at[k]) + (deliver(at[k]) if k == ROUNDS - 1 else []):
                    copy.start()

        for k in range(1, ROUNDS):
            if BUILD[k] == end:
                build(k, wide, narrow, angles, pairs, *tables)

    for k in range(ROUNDS):
        rows = slice(0, ROWS) if k in TWICE else slice(HALF, ROWS)
        sent = leave.at[k, 0:CHUNKS, rows]
        pltpu.make_async_copy(sent, sent, send_sem.at[k]).wait()
    lower = leave.at[ROUNDS - 1, 0:CHUNKS, 0:HALF]
    pltpu.make_async_copy(lower, lower, out_sem).wait()
    pltpu.make_async_copy(lower, lower, last_sem).wait()


def body(state, angles, cz_pairs):
    hbm = pl.BlockSpec(memory_space=pltpu.HBM)
    result = pl.pallas_call(
        kernel,
        out_shape=jax.ShapeDtypeStruct((CHUNKS, ROWS, LANES), F32),
        in_specs=[hbm, hbm, hbm],
        out_specs=pl.BlockSpec(memory_space=pl.ANY),
        scratch_shapes=[
            pltpu.SMEM((ROUNDS, 2, 7), F32),
            pltpu.SMEM((ROUNDS, 2, 12), jnp.int32),
            pltpu.VMEM((ROUNDS, CHUNKS, ROWS, LANES), F32),
            pltpu.VMEM((ROUNDS, CHUNKS, ROWS, LANES), F32),
            pltpu.VMEM((ROUNDS, 2 * ROWS, 2 * LANES), BF16),
            pltpu.VMEM((ROUNDS, 2 * ROWS, 2 * LANES), BF16),
            pltpu.VMEM((ROUNDS, ROWS, LANES), F32),
            pltpu.VMEM((ROUNDS, ROWS, CHUNKS), BF16),
            pltpu.VMEM((ROUNDS, CHUNKS, LANES), F32),
            pltpu.SemaphoreType.DMA((2,)),
            pltpu.SemaphoreType.DMA((GROUPS,)),
            pltpu.SemaphoreType.DMA,
            pltpu.SemaphoreType.DMA,
            pltpu.SemaphoreType.DMA((ROUNDS,)),
            pltpu.SemaphoreType.DMA((ROUNDS - 1, GROUPS)),
        ],
        compiler_params=pltpu.CompilerParams(
            collective_id=0, has_side_effects=True, vmem_limit_bytes=48 << 20
        ),
        name="circuit",
    )(*[pltpu.with_memory_space_constraint(v, pltpu.HBM) for v in (angles, cz_pairs.transpose(0, 2, 1))], pltpu.with_memory_space_constraint(state.reshape(CHUNKS, ROWS, LANES), pltpu.HBM))
    return result.reshape(state.shape)


def solution(mesh):
    return jax.shard_map(
        body,
        mesh=mesh,
        in_specs=(P("wide", "narrow", None), P(), P()),
        out_specs=P("wide", "narrow", None),
        check_vma=False,
    )
```

```python
import functools

import jax
import jax.numpy as jnp
from jax import lax
from jax.experimental import pallas as pl
from jax.experimental.pallas import tpu as pltpu
from jax.sharding import PartitionSpec as P

MESH = pl.DeviceIdType.MESH
F32 = jnp.float32
BF16 = jnp.bfloat16
ROUNDS = 6
ROWS = 128
LANES = 128
HALF = 64
CHUNKS = 32
GROUP = 1
GROUPS = CHUNKS // GROUP
TWICE = (3, 4)
OFFSET = (0, 3, 9, 15, 21, 27)
ORDER = (0, 1, 2, 3, 4, 5)
BUILD = (0, 1, 9, 15, 21, 27)


def trade_bit(k, wide, narrow):
    step, index = 1 << k // 2, (narrow if k % 2 else wide)
    return step, (index // step) % 2


def partner_of(k, wide, narrow):
    step, bit = trade_bit(k, wide, narrow)
    move = step * (1 - 2 * bit)
    return (wide, narrow + move) if k % 2 else (wide + move, narrow)


def beyond(k, wide, narrow):
    return partner_of(k, *partner_of(k - 2, wide, narrow))


def row_order(pos, k, bit):
    low = pos & 63
    under = low & ((1 << k) - 1)
    over = (low >> k) << (k + 1)
    return under | over | (((pos >> 6) ^ bit) << k)


def fold_parity(bits):
    bits = bits ^ (bits >> 4)
    bits = bits ^ (bits >> 2)
    bits = bits ^ (bits >> 1)
    return bits & 1


def rotation_product(out, inp, cosines, sines, base):
    differ = out ^ inp
    value = 1 - 2 * fold_parity(inp & ~out & 127).astype(F32)
    for qubit in range(7):
        row = base + qubit
        value = value * jnp.where((differ >> qubit) & 1 == 0, cosines[row : row + 1], sines[row : row + 1])
    return value


def split(value):
    high = value.astype(BF16)
    low = (value - high.astype(F32)).astype(BF16)
    return high, low


def iota(shape, axis):
    return lax.broadcasted_iota(jnp.int32, shape, axis)


def build(k, wide, narrow, angles, pairs, right_tab, left_tab, sign_tab, row_tab, lane_tab):
    _, bit = trade_bit(k, wide, narrow)
    rows = iota((ROWS, LANES), 0)
    cols = iota((ROWS, LANES), 1)
    slot = iota((16, LANES), 0)
    half = jnp.zeros((16, LANES), F32)
    for block in range(2):
        for qubit in range(7):
            half = jnp.where(slot == block * 8 + qubit, angles[k, block, qubit] * 0.5, half)
    cosines = jnp.cos(half)
    sines = jnp.sin(half)

    high, low = split(rotation_product(cols, rows, cosines, sines, 0))
    both = jnp.concatenate([high, low], axis=1)
    right_tab[k, 0:ROWS, :] = both
    right_tab[k, ROWS : 2 * ROWS, :] = both

    out = row_order(rows, k, bit ^ (1 if k in (1, 2) else 0))
    inp = row_order(cols, k - 1, trade_bit(k - 1, wide, narrow)[1]) if k else cols
    high, low = split(rotation_product(out, inp, cosines, sines, 8))
    left_tab[k, 0:ROWS, :] = jnp.concatenate([high, high], axis=1)
    left_tab[k, ROWS : 2 * ROWS, :] = jnp.concatenate([low, low], axis=1)

    def signs(index):
        parity = jnp.zeros(index.shape, jnp.int32)
        for pair in range(12):
            parity = parity ^ ((index >> pairs[k, 0, pair]) & (index >> pairs[k, 1, pair]))
        return (1 - 2 * (parity & 1)).astype(F32)

    sign_tab[k] = signs(out * 128 + cols)
    by_row = signs(out[:, :CHUNKS] * 128 + cols[:, :CHUNKS] * 16384)
    row_tab[k] = (by_row * by_row[:, 0:1]).astype(BF16)
    by_lane = signs(rows[:CHUNKS] * 16384 + cols[:CHUNKS])
    lane_tab[k] = by_lane * by_lane[0:1, :] * by_lane[:, 0:1]


def gates(taken, slot, right_tab, left_tab, sign_tab, row_tab, lane_tab):
    chunk = iota((CHUNKS, LANES), 0)
    sums = {}
    for k in taken:
        high, low = split(taken[k].reshape(GROUP * ROWS, LANES))
        sums[k] = jnp.dot(jnp.concatenate([high, low], axis=1), right_tab[k], preferred_element_type=F32)
    phase = {}
    for k in taken:
        lanes = lane_tab[k]
        picks = [jnp.where(chunk == slot[k] * GROUP + j, lanes, 0.0) for j in range(GROUP)]
        picks = jnp.concatenate(picks, axis=1).astype(BF16)
        phase[k] = jnp.dot(row_tab[k], picks, preferred_element_type=F32)
    for k in taken:
        high, low = split(sums[k][:, :LANES] + sums[k][:, LANES:])
        beside = [
            jnp.concatenate([part[j * ROWS : (j + 1) * ROWS] for j in range(GROUP)], axis=1) for part in (high, low)
        ]
        sums[k] = jnp.dot(left_tab[k], jnp.concatenate(beside, axis=0), preferred_element_type=F32)
    given = {}
    for k in taken:
        total = sums[k][:ROWS] + sums[k][ROWS:]
        sign = sign_tab[k]
        given[k] = [
            total[:, j * LANES : (j + 1) * LANES] * (sign * phase[k][:, j * LANES : (j + 1) * LANES])
            for j in range(GROUP)
        ]
    return given


def kernel(
    angles_in, pairs_in, state, final, angles, pairs, held, leave, result, right_tab, left_tab, sign_tab, row_tab, lane_tab,
    small_sem, in_sem, out_sem, last_sem, send_sem, recv_sem
):
    wide = lax.axis_index("wide")
    narrow = lax.axis_index("narrow")
    tables = (right_tab, left_tab, sign_tab, row_tab, lane_tab)

    def fetch(g):
        part = pl.ds(g * GROUP, GROUP)
        return pltpu.make_async_copy(state.at[part], held.at[0, part], in_sem.at[g])

    def send(k, part, side, recv, device):
        return pltpu.make_async_remote_copy(
            src_ref=leave.at[k, part, side * HALF : (side + 1) * HALF],
            dst_ref=held.at[k + 1, part, side * HALF : (side + 1) * HALF],
            send_sem=send_sem.at[k],
            recv_sem=recv,
            device_id=device,
            device_id_type=MESH,
        )

    def trade(k, g):
        part, recv = of(g), recv_sem.at[k, g]
        if k in TWICE:
            return [
                send(k, part, 0, recv, partner_of(k - 2, wide, narrow)),
                send(k, part, 1, recv, beyond(k, wide, narrow)),
            ]
        if k < ROUNDS - 1:
            return [send(k, part, 1, recv, partner_of(k, wide, narrow))]
        return [
            pltpu.make_async_remote_copy(
                src_ref=result.at[part, 1],
                dst_ref=final.at[part, :, last_bit],
                send_sem=send_sem.at[k],
                recv_sem=last_sem,
                device_id=partner_of(k, wide, narrow),
                device_id_type=MESH,
            )
        ]

    def arrived(k, g):
        rows = slice(0, ROWS) if k in TWICE else slice(HALF, ROWS)
        pltpu.make_async_copy(leave.at[k, of(g), rows], held.at[k + 1, of(g), rows], recv_sem.at[k, g]).wait()

    def of(g):
        return pl.ds(g * GROUP, GROUP)

    _, last_bit = trade_bit(ROUNDS - 1, wide, narrow)

    def deliver(g):
        return [pltpu.make_async_copy(result.at[of(g), 0], final.at[of(g), :, last_bit], out_sem)]

    small = [pltpu.make_async_copy(angles_in, angles, small_sem.at[0]), pltpu.make_async_copy(pairs_in, pairs, small_sem.at[1])]
    for copy in small:
        copy.start()
    barrier = pltpu.get_barrier_semaphore()
    for k in range(ROUNDS):
        greeted = beyond(k, wide, narrow) if k in TWICE else partner_of(k, wide, narrow)
        pl.semaphore_signal(barrier, inc=1, device_id=greeted, device_id_type=MESH)

    @pl.loop(0, GROUPS)
    def _(g):
        fetch(g).start()

    for copy in small:
        copy.wait()
    build(0, wide, narrow, angles, pairs, *tables)
    edges = sorted({OFFSET[k] + e for k in range(ROUNDS) for e in (0, GROUPS)} | {1})
    for begin, end in zip(edges[:-1], edges[1:]):
        block = [k for k in ORDER if OFFSET[k] <= begin and end <= OFFSET[k] + GROUPS]

        @pl.loop(begin, end)
        def _(step):
            at = {k: step - OFFSET[k] for k in block}
            for k in block:
                if k == 0:
                    fetch(at[k]).wait()
                else:
                    arrived(k - 1, at[k])
            given = gates({k: held[k, of(at[k])] for k in block}, at, *tables)
            for k in block:
                for j in range(GROUP):
                    if k == ROUNDS - 1:
                        result[at[k] * GROUP + j] = given[k][j].reshape(2, 2, 32, LANES)
                    elif k in TWICE:
                        leave[k, at[k] * GROUP + j] = given[k][j]
                    else:
                        leave[k, at[k] * GROUP + j, HALF:ROWS] = given[k][j][HALF:]
                        held[k + 1, at[k] * GROUP + j, 0:HALF] = given[k][j][:HALF]
            if begin == 0:
                pl.semaphore_wait(barrier, ROUNDS)
            for k in block:
                for copy in trade(k, at[k]) + (deliver(at[k]) if k == ROUNDS - 1 else []):
                    copy.start()

        for k in range(1, ROUNDS):
            if BUILD[k] == end:
                build(k, wide, narrow, angles, pairs, *tables)

    for k in range(ROUNDS - 1):
        rows = slice(0, ROWS) if k in TWICE else slice(HALF, ROWS)
        sent = leave.at[k, 0:CHUNKS, rows]
        pltpu.make_async_copy(sent, sent, send_sem.at[k]).wait()
    for semaphore in (send_sem.at[ROUNDS - 1], out_sem, last_sem):
        pltpu.make_async_copy(result.at[:, 0], result.at[:, 1], semaphore).wait()


def body(state, angles, cz_pairs):
    hbm = pl.BlockSpec(memory_space=pltpu.HBM)
    ended = pl.pallas_call(
        kernel,
        out_shape=jax.ShapeDtypeStruct((CHUNKS, 2, 2, 32, LANES), F32),
        in_specs=[hbm, hbm, hbm],
        out_specs=pl.BlockSpec(memory_space=pl.ANY),
        scratch_shapes=[
            pltpu.SMEM((ROUNDS, 2, 7), F32),
            pltpu.SMEM((ROUNDS, 2, 12), jnp.int32),
            pltpu.VMEM((ROUNDS, CHUNKS, ROWS, LANES), F32),
            pltpu.VMEM((ROUNDS - 1, CHUNKS, ROWS, LANES), F32),
            pltpu.VMEM((CHUNKS, 2, 2, 32, LANES), F32),
            pltpu.VMEM((ROUNDS, 2 * ROWS, 2 * LANES), BF16),
            pltpu.VMEM((ROUNDS, 2 * ROWS, 2 * LANES), BF16),
            pltpu.VMEM((ROUNDS, ROWS, LANES), F32),
            pltpu.VMEM((ROUNDS, ROWS, CHUNKS), BF16),
            pltpu.VMEM((ROUNDS, CHUNKS, LANES), F32),
            pltpu.SemaphoreType.DMA((2,)),
            pltpu.SemaphoreType.DMA((GROUPS,)),
            pltpu.SemaphoreType.DMA,
            pltpu.SemaphoreType.DMA,
            pltpu.SemaphoreType.DMA((ROUNDS,)),
            pltpu.SemaphoreType.DMA((ROUNDS - 1, GROUPS)),
        ],
        compiler_params=pltpu.CompilerParams(
            collective_id=0, has_side_effects=True, vmem_limit_bytes=48 << 20
        ),
        name="circuit",
    )(*[pltpu.with_memory_space_constraint(v, pltpu.HBM) for v in (angles, cz_pairs.transpose(0, 2, 1))], pltpu.with_memory_space_constraint(state.reshape(CHUNKS, ROWS, LANES), pltpu.HBM))
    return ended.reshape(state.shape)


def solution(mesh):
    return jax.shard_map(
        body,
        mesh=mesh,
        in_specs=(P("wide", "narrow", None), P(), P()),
        out_specs=P("wide", "narrow", None),
        check_vma=False,
    )
```
